32 devices in a mesh: section: 4 (over x, core), ctx: 8 (over z, y).
Axes of the slice: x: 2, y: 2, z: 4, core: 2. Of those that a mesh axis runs over, the one named last changes fastest.
Arguments:
- queries: bfloat16 [4, 1024, 2048], P('section', 'ctx'), may hold values from -6 to 6
- keys: bfloat16 [4, 1024, 512], P('section', 'ctx'), may hold values from -6 to 6
- values: bfloat16 [4, 1024, 512], P('section', 'ctx'), may hold values from -6 to 6
- outputs: bfloat16 [4, 1024, 2048], P('section', 'ctx'), may hold values from -2 to 2
- upstream: bfloat16 [4, 1024, 2048], P('section', 'ctx'), may hold values from -6 to 6
- lse: float32 [4, 16, 1024], P('section', None, 'ctx'), may hold values from 3 to 6
- span_ids: int32 [16], P('ctx'), may hold values from 0 to 15, as said below
Outputs:
- grad_queries: bfloat16 [4, 1024, 2048], P('section', 'ctx')
- window_key_gradient: bfloat16 [4, 1024, 512], P('section', 'ctx')
- window_value_gradient: bfloat16 [4, 1024, 512], P('section', 'ctx')
The draws below stay inside these ranges and needn't reach their ends.
Inputs may be any that keep to these rules, and one draw needn't show every extreme that they name: `span_ids`: for each shard n, entries 2 n and 2 n + 1 are c and 15 - c for some c < 8; every span appears once.
All inputs are finite; a program needn't handle non-finite values.
Results may differ from the reference program's by a relative error of at most 0.0051.
Values may be sent and summed in bfloat16 or wider, within the bound.
A program may use at most 64 MiB of HBM per device.

```python
import jax
import jax.numpy as jnp
from jax import lax

QUERY_HEADS = 16
KEY_VALUE_HEADS = 4
HEAD_WIDTH = 128
TOKENS_PER_SHARD = 128
CYCLE = 4
SPAN = 64
SPANS = 16
SEQUENCE_TOKENS = 1024
RELAY_SECTIONS = 4
N_CTX = 8


def draw_span_ids(key, part):
    lower = jax.random.permutation(key, SPANS // 2).astype(jnp.int32)
    upper = (SPANS - 1 - lower).astype(jnp.int32)
    return jnp.stack([lower, upper], axis=1).reshape(SPANS).astype(jnp.int32)


def block_levels(rng, shape, pieces, smallest, top_value):
    level = 1.0
    for dim, blocks in pieces:
        heights = jax.random.uniform(jax.random.fold_in(jax.random.fold_in(rng, 6), dim), (blocks,), jnp.float32, smallest / len(pieces), top_value / len(pieces))
        level = level * jnp.repeat(jnp.exp(heights), shape[dim] // blocks).reshape((-1,) + (1,) * (len(shape) - 1 - dim))
    return level


def gaussian(stream_key, extent, spread, limit, cuts=(), dtype=jnp.bfloat16):
    values = jax.random.normal(stream_key, extent, jnp.float32) * spread
    if len(cuts) > 0:
        values = block_levels(stream_key, extent, cuts, -0.22, 0.18) * values
    return jnp.clip(values, min=-limit, max=limit).astype(dtype)


def setup_inputs(seed: int = 0) -> dict:
    arg_keys = jax.random.split(jax.random.key(seed), 8)
    queries = gaussian(arg_keys[0], (RELAY_SECTIONS, SEQUENCE_TOKENS, QUERY_HEADS * HEAD_WIDTH), 1.0, 6.0, ((0, 4), (1, 8)))
    keys = gaussian(arg_keys[1], (RELAY_SECTIONS, SEQUENCE_TOKENS, KEY_VALUE_HEADS * HEAD_WIDTH), 1.0, 6.0, ((0, 4), (1, 8)))
    values = gaussian(arg_keys[2], (RELAY_SECTIONS, SEQUENCE_TOKENS, KEY_VALUE_HEADS * HEAD_WIDTH), 1.0, 6.0, ((0, 4), (1, 8)))
    outputs = gaussian(arg_keys[3], (RELAY_SECTIONS, SEQUENCE_TOKENS, QUERY_HEADS * HEAD_WIDTH), 0.3, 2.0, ((0, 4), (1, 8)))
    upstream = gaussian(arg_keys[4], (RELAY_SECTIONS, SEQUENCE_TOKENS, QUERY_HEADS * HEAD_WIDTH), 1.0, 6.0, ((0, 4), (1, 8)))
    lse = jnp.clip(3.0 + 3.0 * jax.random.uniform(arg_keys[5], (RELAY_SECTIONS, QUERY_HEADS, SEQUENCE_TOKENS), jnp.float32) ** block_levels(arg_keys[5], (RELAY_SECTIONS, QUERY_HEADS, SEQUENCE_TOKENS), ((0, 4), (2, 8)), -0.2, 0.2), 3.0, 6.0)
    span_ids = draw_span_ids(jax.random.fold_in(arg_keys[7], 71), 0)
    return {"queries": queries, "keys": keys, "values": values, "outputs": outputs, "upstream": upstream, "lse": lse, "span_ids": span_ids}


def token_positions(span_ids):
    local = jnp.arange(TOKENS_PER_SHARD)
    pairs = span_ids.reshape(N_CTX, 2)
    chosen = pairs[:, local // SPAN]
    return (chosen * SPAN + local % SPAN).astype(jnp.int32)


def section_grads(queries, keys, values, outputs, output_gradient, lse, positions):
    query_group = QUERY_HEADS // KEY_VALUE_HEADS
    scale = HEAD_WIDTH ** -0.5
    head_queries = queries.reshape(N_CTX, TOKENS_PER_SHARD, KEY_VALUE_HEADS, query_group, HEAD_WIDTH).astype(jnp.float32)
    head_gradient = output_gradient.reshape(N_CTX, TOKENS_PER_SHARD, KEY_VALUE_HEADS, query_group, HEAD_WIDTH).astype(jnp.float32)
    head_output = outputs.reshape(N_CTX, TOKENS_PER_SHARD, KEY_VALUE_HEADS, query_group, HEAD_WIDTH).astype(jnp.float32)
    head_keys = keys.reshape(N_CTX, TOKENS_PER_SHARD, KEY_VALUE_HEADS, HEAD_WIDTH).astype(jnp.float32)
    head_values = values.reshape(N_CTX, TOKENS_PER_SHARD, KEY_VALUE_HEADS, HEAD_WIDTH).astype(jnp.float32)
    delta = jnp.einsum('nqhgd,nqhgd->nhgq', head_gradient, head_output)
    row_logsumexp = lse.reshape(KEY_VALUE_HEADS, query_group, N_CTX, TOKENS_PER_SHARD).transpose(2, 0, 1, 3)
    query_gradient = jnp.zeros(head_queries.shape, jnp.float32)
    key_gradient = jnp.zeros(head_keys.shape, jnp.float32)
    value_gradient = jnp.zeros(head_keys.shape, jnp.float32)
    for step in range(CYCLE + 1):
        key_now = jnp.roll(head_keys, step, 0)
        value_now = jnp.roll(head_values, step, 0)
        key_pos = jnp.roll(positions, step, 0)
        score = jnp.einsum('nqhgd,nkhd->nhgqk', head_queries, key_now) * scale
        allowed = key_pos[:, None, None, None, :] <= positions[:, None, None, :, None]
        prob = jnp.where(allowed, jnp.exp(score - row_logsumexp[..., None]), jnp.float32(0.0))
        prob_b = lax.optimization_barrier(prob.astype(jnp.bfloat16)).astype(jnp.float32)
        dvalue = jnp.einsum('nhgqk,nqhgd->nkhd', prob_b, head_gradient)
        dprob = jnp.einsum('nqhgd,nkhd->nhgqk', head_gradient, value_now)
        dscore = prob * (dprob - delta[..., None]) * scale
        dscore_b = lax.optimization_barrier(dscore.astype(jnp.bfloat16)).astype(jnp.float32)
        query_gradient = query_gradient + jnp.einsum('nhgqk,nkhd->nqhgd', dscore_b, key_now)
        dkey = jnp.einsum('nhgqk,nqhgd->nkhd', dscore_b, head_queries)
        key_gradient = key_gradient + jnp.roll(dkey, -step, 0)
        value_gradient = value_gradient + jnp.roll(dvalue, -step, 0)
    return (query_gradient.reshape(SEQUENCE_TOKENS, QUERY_HEADS * HEAD_WIDTH).astype(jnp.bfloat16),
            key_gradient.reshape(SEQUENCE_TOKENS, KEY_VALUE_HEADS * HEAD_WIDTH).astype(jnp.bfloat16),
            value_gradient.reshape(SEQUENCE_TOKENS, KEY_VALUE_HEADS * HEAD_WIDTH).astype(jnp.bfloat16))


def reference(queries, keys, values, outputs, upstream, lse, span_ids):
    positions = token_positions(span_ids)
    output_gradient = jnp.roll(upstream, -1, 0)

    def one_section(items):
        return section_grads(items[0], items[1], items[2], items[3], items[4], items[5], positions)

    query_gradient, key_gradient, value_gradient = lax.map(one_section, (queries, keys, values, outputs, output_gradient, lse))
    return (query_gradient, key_gradient, value_gradient)
```

```python
import functools
import math

import jax
import jax.numpy as jnp
from jax import lax
from jax.experimental import pallas as pl
from jax.experimental.pallas import tpu as pltpu
from jax.sharding import PartitionSpec as P

G = 4
R = 4
D = 128
HEAD = 16
MESH = pl.DeviceIdType.MESH
F32 = jnp.float32
BF16 = jnp.bfloat16
C1, C2, X1, X3 = 0, 1, 2, 3


def dot(a, b, ca, cb):
    return lax.dot_general(a, b, (((ca,), (cb,)), ((), ())), preferred_element_type=F32)


def kernel(
    sections, count, span_ref, q_ref, k_ref, v_ref, o_ref, lse_ref, up_ref,
    dq_ref, dk_ref, dv_ref,
    kv, do, dqt, delta, pacc, gsend, grecv,
    up_s, up_r, kv_s, kv_r, g_s, g_r,
):
    T = q_ref.shape[1]
    half = T // 2
    sec = lax.axis_index("section")
    me = lax.axis_index("ctx")
    side = lax.rem(me, 2)
    sec_prev = lax.rem(sec + sections - 1, sections)
    sec_next = lax.rem(sec + 1, sections)
    above = lax.rem(me + 2, count)
    below = lax.rem(me + count - 2, count)
    partner = me + 1 - 2 * side

    s0 = span_ref[0]
    s1 = span_ref[1]

    rows = lax.broadcasted_iota(jnp.int32, (HEAD, D), 0)
    header = jnp.where(rows < HEAD // 2, s0, s1).astype(F32).astype(BF16)
    for g in range(G):
        kv[0, g, 0:HEAD, :] = header
        kv[0, g, HEAD : HEAD + T, :] = k_ref[0, :, g * D : (g + 1) * D]
        kv[0, g, HEAD + T : HEAD + 2 * T, :] = v_ref[0, :, g * D : (g + 1) * D]

    barrier = pltpu.get_barrier_semaphore()
    for axis, other in (
        ("ctx", above), ("ctx", below), ("ctx", partner),
        ("section", sec_prev), ("section", sec_next),
    ):
        pl.semaphore_signal(barrier, inc=1, device_id={axis: other}, device_id_type=MESH)
    pl.semaphore_wait(barrier, 5)

    def up_copy(g):
        return pltpu.make_async_remote_copy(
            src_ref=up_ref.at[0, :, pl.ds(pl.multiple_of(g * (R * D), R * D), R * D)],
            dst_ref=do.at[g], send_sem=up_s.at[g], recv_sem=up_r.at[g],
            device_id={"section": sec_prev}, device_id_type=MESH,
        )

    def kv_copy(t, src, g):
        return pltpu.make_async_remote_copy(
            src_ref=kv.at[src, g], dst_ref=kv.at[t + 1, g],
            send_sem=kv_s.at[t, g], recv_sem=kv_r.at[t, g],
            device_id={"ctx": above if t in (C1, C2) else partner}, device_id_type=MESH,
        )

    def g_copy(t, g):
        return pltpu.make_async_remote_copy(
            src_ref=gsend.at[t, g], dst_ref=grecv.at[t, g],
            send_sem=g_s.at[t, g], recv_sem=g_r.at[t, g],
            device_id={"ctx": below if t in (C1, C2) else partner}, device_id_type=MESH,
        )

    def loop(body):
        def step(g, carry):
            body(g)
            return carry

        lax.fori_loop(0, G, step, 0)

    def start_all(g):
        kv_copy(C1, 0, g).start()

        @pl.when(side == 0)
        def _():
            kv_copy(X1, 0, g).start()

        up_copy(g).start()

    loop(start_all)

    scale = D ** (-0.5)
    scale2 = scale * math.log2(math.e)
    krow = lax.broadcasted_iota(jnp.int32, (T, D), 0)
    kbase = jnp.where(krow < half, krow, krow - half).astype(F32)
    qlane = lax.broadcasted_iota(jnp.int32, (T, T), 1)
    qpos = (jnp.where(qlane < half, s0, s1) * half).astype(F32) + jnp.where(
        qlane < half, qlane, qlane - half
    ).astype(F32)

    def heads(ref, *at):
        return jnp.concatenate([ref[at + (slice(None), slice(j * D, (j + 1) * D))] for j in range(R)], axis=0)

    def q_heads(g):
        wide = q_ref[0, :, pl.ds(pl.multiple_of(g * (R * D), R * D), R * D)]
        return jnp.concatenate([wide[:, j * D : (j + 1) * D] for j in range(R)], axis=0)

    def block(g, slot, first=False):
        head = kv[slot, g, 0:HEAD, :].astype(F32)
        k = kv[slot, g, HEAD : HEAD + T, :]
        v = kv[slot, g, HEAD + T : HEAD + 2 * T, :]
        q4 = q_heads(g)
        do4 = heads(do, g)
        kpos = jnp.where(krow < half, head[0:1, :], head[8:9, :]) * half + kbase
        allowed = kpos <= qpos
        lse = jnp.concatenate(
            [lse_ref[0, pl.ds(g * R + j, 1), :] for j in range(R)], axis=1
        ) * math.log2(math.e)
        dl = delta[g, 0:1, :]
        s = dot(k, q4, 1, 1)
        e = jnp.exp2(s * scale2 - lse)
        p = jnp.where(jnp.concatenate([allowed] * R, axis=1), e, 0.0)
        dp = dot(v, do4, 1, 1)
        ds = (p * (dp - dl) * scale).astype(BF16)
        dval = dot(p.astype(BF16), do4, 1, 0)
        dkey = dot(ds, q4, 1, 0)
        term = dot(k, ds, 0, 0)
        if first:
            dqt[g] = term
        else:
            dqt[g] += term
        return dkey, dval

    def keep(g, slot, pair):
        pacc[slot, g, 0:T, :] = pair[0]
        pacc[slot, g, T : 2 * T, :] = pair[1]

    def pass_on(t, g, pair):
        gsend[t, g, 0:T, :] = pair[0].astype(BF16)
        gsend[t, g, T : 2 * T, :] = pair[1].astype(BF16)
        g_copy(t, g).start()

    def phase1(g):
        kv_copy(C1, 0, g).wait_recv()
        kv_copy(C2, 1, g).start()

        @pl.when(side == 0)
        def _():
            kv_copy(X3, 1, g).start()

        @pl.when(side == 1)
        def _():
            kv_copy(X1, 1, g).start()

        up_copy(g).wait_recv()
        o4 = o_ref[0, :, pl.ds(pl.multiple_of(g * (R * D), R * D), R * D)].astype(F32)
        prod = o4 * do[g].astype(F32)
        delta[g, 0:1, :] = jnp.concatenate(
            [jnp.sum(prod[:, j * D : (j + 1) * D].T, axis=0, keepdims=True) for j in range(R)], axis=1
        )
        keep(g, 0, block(g, 0, True))

    loop(phase1)

    def phase2(g):
        kv_copy(C2, 1, g).wait_recv()

        @pl.when(side == 1)
        def _():
            kv_copy(X3, 2, g).start()

        keep(g, 1, block(g, 1))

    loop(phase2)

    def phase3(g):
        kv_copy(X1, 0, g).wait_recv()
        pass_on(X1, g, block(g, 3))
        kv_copy(X3, 0, g).wait_recv()
        pass_on(X3, g, block(g, 4))
        keep(g, 2, block(g, 2))
        total = dqt[g]
        dq_ref[0, :, pl.ds(pl.multiple_of(g * (R * D), R * D), R * D)] = jnp.concatenate(
            [total[:, j * T : (j + 1) * T].T for j in range(R)], axis=1
        ).astype(BF16)

    loop(phase3)

    def phase4(g):
        g_copy(X1, g).wait_recv()
        pacc[side, g] += grecv[X1, g].astype(F32)
        g_copy(X3, g).wait_recv()
        pacc[side + 1, g] += grecv[X3, g].astype(F32)
        gsend[C2, g] = pacc[2, g].astype(BF16)
        g_copy(C2, g).start()

    loop(phase4)

    def phase5(g):
        g_copy(C2, g).wait_recv()
        gsend[C1, g] = (pacc[1, g] + grecv[C2, g].astype(F32)).astype(BF16)
        g_copy(C1, g).start()

    loop(phase5)

    def phase6(g):
        g_copy(C1, g).wait_recv()
        total = (pacc[0, g] + grecv[C1, g].astype(F32)).astype(BF16)
        at = pl.ds(pl.multiple_of(g * D, D), D)
        dk_ref[0, :, at] = total[0:T]
        dv_ref[0, :, at] = total[T : 2 * T]

    loop(phase6)

    def finish(g):
        up_copy(g).wait_send()
        for t in (C1, C2, X1, X3):
            kv_copy(t, 0, g).wait_send()
            g_copy(t, g).wait_send()

    loop(finish)


def body(mesh, queries, keys, values, outputs, upstream, lse, span_ids):
    T = queries.shape[1]
    rows = HEAD + 2 * T
    vmem = pl.BlockSpec(memory_space=pltpu.VMEM)
    return pl.pallas_call(
        functools.partial(kernel, mesh.shape["section"], mesh.shape["ctx"]),
        out_shape=(
            jax.ShapeDtypeStruct(queries.shape, BF16),
            jax.ShapeDtypeStruct(keys.shape, BF16),
            jax.ShapeDtypeStruct(values.shape, BF16),
        ),
        in_specs=[pl.BlockSpec(memory_space=pltpu.SMEM)] + [vmem] * 5 + [pl.BlockSpec(memory_space=pl.ANY)],
        out_specs=(vmem, vmem, vmem),
        scratch_shapes=[
            pltpu.VMEM((5, G, rows, D), BF16),
            pltpu.VMEM((G, T, R * D), BF16),
            pltpu.VMEM((G, D, R * T), F32),
            pltpu.VMEM((G, 8, R * T), F32),
            pltpu.VMEM((3, G, 2 * T, D), F32),
            pltpu.VMEM((4, G, 2 * T, D), BF16),
            pltpu.VMEM((4, G, 2 * T, D), BF16),
            pltpu.SemaphoreType.DMA((G,)),
            pltpu.SemaphoreType.DMA((G,)),
            pltpu.SemaphoreType.DMA((4, G)),
            pltpu.SemaphoreType.DMA((4, G)),
            pltpu.SemaphoreType.DMA((4, G)),
            pltpu.SemaphoreType.DMA((4, G)),
        ],
        compiler_params=pltpu.CompilerParams(
            collective_id=0, has_side_effects=True, vmem_limit_bytes=40 * 1024 * 1024
        ),
    )(span_ids, queries, keys, values, outputs, lse, upstream)


def solution(mesh):
    placed = (
        P("section", "ctx", None),
        P("section", "ctx", None),
        P("section", "ctx", None),
        P("section", "ctx", None),
        P("section", "ctx", None),
        P("section", None, "ctx"),
        P("ctx"),
    )
    return jax.shard_map(
        functools.partial(body, mesh),
        mesh=mesh,
        in_specs=placed,
        out_specs=(P("section", "ctx", None), P("section", "ctx", None), P("section", "ctx", None)),
        check_vma=False,
    )
```

```python
import functools
import math

import jax
import jax.numpy as jnp
from jax import lax
from jax.experimental import pallas as pl
from jax.experimental.pallas import tpu as pltpu
from jax.sharding import PartitionSpec as P

G = 4
R = 4
D = 128
HEAD = 16
MESH = pl.DeviceIdType.MESH
F32 = jnp.float32
BF16 = jnp.bfloat16
C1, C2, X1, X3 = 0, 1, 2, 3


def dot(a, b, ca, cb):
    return lax.dot_general(a, b, (((ca,), (cb,)), ((), ())), preferred_element_type=F32)


def kernel(
    sections, count, span_ref, q_hbm, k_hbm, v_hbm, o_hbm, lse_hbm, up_ref,
    dq_ref, dk_ref, dv_ref,
    q_ref, o_ref, lse_ref,
    kv, do, dqt, delta, pacc, gsend, grecv,
    loc, kvloc, up_s, up_r, kv_s, kv_r, g_s, g_r,
):
    T = q_ref.shape[1]
    half = T // 2
    sec = lax.axis_index("section")
    me = lax.axis_index("ctx")
    side = lax.rem(me, 2)
    sec_prev = lax.rem(sec + sections - 1, sections)
    sec_next = lax.rem(sec + 1, sections)
    above = lax.rem(me + 2, count)
    below = lax.rem(me + count - 2, count)
    partner = me + 1 - 2 * side

    barrier = pltpu.get_barrier_semaphore()
    for axis, other in (
        ("ctx", above), ("ctx", below), ("ctx", partner),
        ("section", sec_prev), ("section", sec_next),
    ):
        pl.semaphore_signal(barrier, inc=1, device_id={axis: other}, device_id_type=MESH)

    own = []
    for g in range(G):
        cols = slice(g * D, (g + 1) * D)
        own.append((
            pltpu.make_async_copy(k_hbm.at[0, :, cols], kv.at[0, g, HEAD : HEAD + T, :], kvloc.at[0, g]),
            pltpu.make_async_copy(v_hbm.at[0, :, cols], kv.at[0, g, HEAD + T : HEAD + 2 * T, :], kvloc.at[1, g]),
        ))
        own[g][0].start()
        own[g][1].start()
    local = (
        pltpu.make_async_copy(q_hbm, q_ref, loc.at[0]),
        pltpu.make_async_copy(o_hbm, o_ref, loc.at[1]),
        pltpu.make_async_copy(lse_hbm, lse_ref, loc.at[2]),
    )
    for copy in local:
        copy.start()

    s0 = span_ref[0]
    s1 = span_ref[1]
    rows = lax.broadcasted_iota(jnp.int32, (HEAD, D), 0)
    header = jnp.where(rows < HEAD // 2, s0, s1).astype(F32).astype(BF16)
    for g in range(G):
        kv[0, g, 0:HEAD, :] = header
    pl.semaphore_wait(barrier, 5)

    def up_copy(g):
        return pltpu.make_async_remote_copy(
            src_ref=up_ref.at[0, :, pl.ds(pl.multiple_of(g * (R * D), R * D), R * D)],
            dst_ref=do.at[g], send_sem=up_s.at[g], recv_sem=up_r.at[g],
            device_id={"section": sec_prev}, device_id_type=MESH,
        )

    def kv_copy(t, src, g):
        return pltpu.make_async_remote_copy(
            src_ref=kv.at[src, g], dst_ref=kv.at[t + 1, g],
            send_sem=kv_s.at[t, g], recv_sem=kv_r.at[t, g],
            device_id={"ctx": above if t in (C1, C2) else partner}, device_id_type=MESH,
        )

    def g_copy(t, g):
        return pltpu.make_async_remote_copy(
            src_ref=gsend.at[t, g], dst_ref=grecv.at[t, g],
            send_sem=g_s.at[t, g], recv_sem=g_r.at[t, g],
            device_id={"ctx": below if t in (C1, C2) else partner}, device_id_type=MESH,
        )

    def send_own(g):
        kv_copy(C1, 0, g).start()

        @pl.when(side == 0)
        def _():
            kv_copy(X1, 0, g).start()

    for g in range(G):
        own[g][0].wait()
        own[g][1].wait()
        if g < 2:
            send_own(g)
        up_copy(g).start()
    for copy in local:
        copy.wait()

    scale = D ** (-0.5)
    scale2 = scale * math.log2(math.e)
    krow = lax.broadcasted_iota(jnp.int32, (T, D), 0)
    kbase = jnp.where(krow < half, krow, krow - half).astype(F32)
    qlane = lax.broadcasted_iota(jnp.int32, (T, T), 1)
    qpos = (jnp.where(qlane < half, s0, s1) * half).astype(F32) + jnp.where(
        qlane < half, qlane, qlane - half
    ).astype(F32)

    def heads(ref, *at):
        return jnp.concatenate([ref[at + (slice(None), slice(j * D, (j + 1) * D))] for j in range(R)], axis=0)

    def q_heads(g):
        wide = q_ref[0, :, pl.ds(pl.multiple_of(g * (R * D), R * D), R * D)]
        return jnp.concatenate([wide[:, j * D : (j + 1) * D] for j in range(R)], axis=0)

    def block(g, slot, first=False):
        head = kv[slot, g, 0:HEAD, :].astype(F32)
        k = kv[slot, g, HEAD : HEAD + T, :]
        v = kv[slot, g, HEAD + T : HEAD + 2 * T, :]
        q4 = q_heads(g)
        do4 = heads(do, g)
        kpos = jnp.where(krow < half, head[0:1, :], head[8:9, :]) * half + kbase
        allowed = kpos <= qpos
        lse = jnp.concatenate(
            [lse_ref[0, pl.ds(g * R + j, 1), :] for j in range(R)], axis=1
        ) * math.log2(math.e)
        dl = delta[g, 0:1, :]
        s = dot(k, q4, 1, 1)
        e = jnp.exp2(s * scale2 - lse)
        p = jnp.where(jnp.concatenate([allowed] * R, axis=1), e, 0.0)
        dp = dot(v, do4, 1, 1)
        ds = (p * (dp - dl) * scale).astype(BF16)
        dval = dot(p.astype(BF16), do4, 1, 0)
        dkey = dot(ds, q4, 1, 0)
        term = dot(k, ds, 0, 0)
        if first:
            dqt[g] = term
        else:
            dqt[g] += term
        return dkey, dval

    def keep(g, slot, pair):
        pacc[slot, g, 0:T, :] = pair[0]
        pacc[slot, g, T : 2 * T, :] = pair[1]

    def pass_on(t, g, pair):
        gsend[t, g, 0:T, :] = pair[0].astype(BF16)
        gsend[t, g, T : 2 * T, :] = pair[1].astype(BF16)
        g_copy(t, g).start()

    def relay(g):
        kv_copy(C1, 0, g).wait_recv()
        kv_copy(C2, 1, g).start()

        @pl.when(side == 0)
        def _():
            kv_copy(X3, 1, g).start()

        @pl.when(side == 1)
        def _():
            kv_copy(X1, 1, g).start()

        @pl.when(g + 2 < G)
        def _():
            send_own(g + 2)

    def work(g):
        kv_copy(C2, 1, g).wait_recv()

        @pl.when(side == 1)
        def _():
            kv_copy(X3, 2, g).start()

        up_copy(g).wait_recv()
        o4 = o_ref[0, :, pl.ds(pl.multiple_of(g * (R * D), R * D), R * D)].astype(F32)
        prod = o4 * do[g].astype(F32)
        delta[g, 0:1, :] = jnp.concatenate(
            [jnp.sum(prod[:, j * D : (j + 1) * D].T, axis=0, keepdims=True) for j in range(R)], axis=1
        )
        keep(g, 0, block(g, 0, True))
        keep(g, 1, block(g, 1))
        keep(g, 2, block(g, 2))
        kv_copy(X1, 0, g).wait_recv()
        pass_on(X1, g, block(g, 3))
        kv_copy(X3, 0, g).wait_recv()
        pass_on(X3, g, block(g, 4))
        total = dqt[g]
        dq_ref[0, :, pl.ds(pl.multiple_of(g * (R * D), R * D), R * D)] = jnp.concatenate(
            [total[:, j * T : (j + 1) * T].T for j in range(R)], axis=1
        ).astype(BF16)

    def join(g):
        g_copy(X1, g).wait_recv()
        pacc[side, g] += grecv[X1, g].astype(F32)
        g_copy(X3, g).wait_recv()
        pacc[side + 1, g] += grecv[X3, g].astype(F32)
        gsend[C2, g] = pacc[2, g].astype(BF16)
        g_copy(C2, g).start()

    def descend(g):
        g_copy(C2, g).wait_recv()
        gsend[C1, g] = (pacc[1, g] + grecv[C2, g].astype(F32)).astype(BF16)
        g_copy(C1, g).start()

    def home(g):
        g_copy(C1, g).wait_recv()
        total = (pacc[0, g] + grecv[C1, g].astype(F32)).astype(BF16)
        at = pl.ds(pl.multiple_of(g * D, D), D)
        dk_ref[0, :, at] = total[0:T]
        dv_ref[0, :, at] = total[T : 2 * T]

    def step(i, carry):
        for lag, stage in enumerate((relay, work, join, descend, home)):
            g = i - lag

            @pl.when((g >= 0) & (g < G))
            def _():
                stage(g)

        return carry

    lax.fori_loop(0, G + 4, step, 0)

    def finish(g, carry):
        up_copy(g).wait_send()
        for t in (C1, C2, X1, X3):
            kv_copy(t, 0, g).wait_send()
            g_copy(t, g).wait_send()
        return carry

    lax.fori_loop(0, G, finish, 0)


def body(mesh, queries, keys, values, outputs, upstream, lse, span_ids):
    T = queries.shape[1]
    rows = HEAD + 2 * T
    vmem = pl.BlockSpec(memory_space=pltpu.VMEM)
    return pl.pallas_call(
        functools.partial(kernel, mesh.shape["section"], mesh.shape["ctx"]),
        out_shape=(
            jax.ShapeDtypeStruct(queries.shape, BF16),
            jax.ShapeDtypeStruct(keys.shape, BF16),
            jax.ShapeDtypeStruct(values.shape, BF16),
        ),
        in_specs=[pl.BlockSpec(memory_space=pltpu.SMEM)] + [pl.BlockSpec(memory_space=pltpu.HBM)] * 6,
        out_specs=(vmem, vmem, vmem),
        scratch_shapes=[
            pltpu.VMEM(queries.shape, BF16),
            pltpu.VMEM(outputs.shape, BF16),
            pltpu.VMEM(lse.shape, F32),
            pltpu.VMEM((5, G, rows, D), BF16),
            pltpu.VMEM((G, T, R * D), BF16),
            pltpu.VMEM((G, D, R * T), F32),
            pltpu.VMEM((G, 8, R * T), F32),
            pltpu.VMEM((3, G, 2 * T, D), F32),
            pltpu.VMEM((4, G, 2 * T, D), BF16),
            pltpu.VMEM((4, G, 2 * T, D), BF16),
            pltpu.SemaphoreType.DMA((3,)),
            pltpu.SemaphoreType.DMA((2, G)),
            pltpu.SemaphoreType.DMA((G,)),
            pltpu.SemaphoreType.DMA((G,)),
            pltpu.SemaphoreType.DMA((4, G)),
            pltpu.SemaphoreType.DMA((4, G)),
            pltpu.SemaphoreType.DMA((4, G)),
            pltpu.SemaphoreType.DMA((4, G)),
        ],
        compiler_params=pltpu.CompilerParams(
            collective_id=0, has_side_effects=True, vmem_limit_bytes=60 * 1024 * 1024
        ),
    )(span_ids, queries, keys, values, outputs, lse, upstream)


def solution(mesh):
    placed = (
        P("section", "ctx", None),
        P("section", "ctx", None),
        P("section", "ctx", None),
        P("section", "ctx", None),
        P("section", "ctx", None),
        P("section", None, "ctx"),
        P("ctx"),
    )
    return jax.shard_map(
        functools.partial(body, mesh),
        mesh=mesh,
        in_specs=placed,
        out_specs=(P("section", "ctx", None), P("section", "ctx", None), P("section", "ctx", None)),
        check_vma=False,
    )
```

```python
import functools
import math

import jax
import jax.numpy as jnp
from jax import lax
from jax.experimental import pallas as pl
from jax.experimental.pallas import tpu as pltpu
from jax.sharding import PartitionSpec as P

G = 4
R = 4
D = 128
AHEAD = 4
HEAD = 16
ORDER = (
    ("a", 0), ("a", 1), ("a", 2), ("a", 3), ("b", 0), ("b", 1), ("b", 2), ("b", 3), ("w", 0), ("w", 1), ("j", 0), ("w", 2), ("j", 1), ("d", 0), ("w", 3), ("j", 2), ("d", 1), ("j", 3), ("d", 2), ("h", 0), ("d", 3), ("h", 1), ("h", 2), ("h", 3),
)
MESH = pl.DeviceIdType.MESH
F32 = jnp.float32
BF16 = jnp.bfloat16
C1, C2, X1, X3 = 0, 1, 2, 3


def dot(a, b, ca, cb):
    return lax.dot_general(a, b, (((ca,), (cb,)), ((), ())), preferred_element_type=F32)


def kernel(
    sections, count, span_ref, q_hbm, k_hbm, v_hbm, o_hbm, lse_hbm, up_ref,
    dq_ref, dk_ref, dv_ref,
    q_ref, o_ref, lse_ref,
    kv, do, dqt, delta, pacc, gsend, grecv,
    loc, kvloc, up_s, up_r, kv_s, kv_r, g_s, g_r,
):
    T = q_ref.shape[1]
    half = T // 2
    sec = lax.axis_index("section")
    me = lax.axis_index("ctx")
    side = lax.rem(me, 2)
    sec_prev = lax.rem(sec + sections - 1, sections)
    sec_next = lax.rem(sec + 1, sections)
    above = lax.rem(me + 2, count)
    below = lax.rem(me + count - 2, count)
    partner = me + 1 - 2 * side

    barrier = pltpu.get_barrier_semaphore()
    for axis, other in (
        ("ctx", above), ("ctx", below), ("ctx", partner),
        ("section", sec_prev), ("section", sec_next),
    ):
        pl.semaphore_signal(barrier, inc=1, device_id={axis: other}, device_id_type=MESH)

    own = []
    for g in range(G):
        cols = slice(g * D, (g + 1) * D)
        own.append((
            pltpu.make_async_copy(k_hbm.at[0, :, cols], kv.at[0, g, HEAD : HEAD + T, :], kvloc.at[0, g]),
            pltpu.make_async_copy(v_hbm.at[0, :, cols], kv.at[0, g, HEAD + T : HEAD + 2 * T, :], kvloc.at[1, g]),
        ))
        own[g][0].start()
        own[g][1].start()
    local = (
        pltpu.make_async_copy(q_hbm, q_ref, loc.at[0]),
        pltpu.make_async_copy(o_hbm, o_ref, loc.at[1]),
        pltpu.make_async_copy(lse_hbm, lse_ref, loc.at[2]),
    )
    for copy in local:
        copy.start()

    s0 = span_ref[0]
    s1 = span_ref[1]
    rows = lax.broadcasted_iota(jnp.int32, (HEAD, D), 0)
    header = jnp.where(rows < HEAD // 2, s0, s1).astype(F32).astype(BF16)
    for g in range(G):
        kv[0, g, 0:HEAD, :] = header
    pl.semaphore_wait(barrier, 5)

    def up_copy(g):
        return pltpu.make_async_remote_copy(
            src_ref=up_ref.at[0, :, pl.ds(pl.multiple_of(g * (R * D), R * D), R * D)],
            dst_ref=do.at[g], send_sem=up_s.at[g], recv_sem=up_r.at[g],
            device_id={"section": sec_prev}, device_id_type=MESH,
        )

    def kv_copy(t, src, g):
        return pltpu.make_async_remote_copy(
            src_ref=kv.at[src, g], dst_ref=kv.at[t + 1, g],
            send_sem=kv_s.at[t, g], recv_sem=kv_r.at[t, g],
            device_id={"ctx": above if t in (C1, C2) else partner}, device_id_type=MESH,
        )

    def g_copy(t, g):
        return pltpu.make_async_remote_copy(
            src_ref=gsend.at[t, g], dst_ref=grecv.at[t, g],
            send_sem=g_s.at[t, g], recv_sem=g_r.at[t, g],
            device_id={"ctx": below if t in (C1, C2) else partner}, device_id_type=MESH,
        )

    def send_own(g):
        kv_copy(C1, 0, g).start()

        @pl.when(side == 0)
        def _():
            kv_copy(X1, 0, g).start()

    for g in range(G):
        own[g][0].wait()
        own[g][1].wait()
        if g < AHEAD:
            send_own(g)
        up_copy(g).start()
    for copy in local:
        copy.wait()

    scale = D ** (-0.5)
    scale2 = scale * math.log2(math.e)
    krow = lax.broadcasted_iota(jnp.int32, (T, D), 0)
    kbase = jnp.where(krow < half, krow, krow - half).astype(F32)
    qlane = lax.broadcasted_iota(jnp.int32, (T, T), 1)
    qpos = (jnp.where(qlane < half, s0, s1) * half).astype(F32) + jnp.where(
        qlane < half, qlane, qlane - half
    ).astype(F32)

    def heads(ref, *at):
        return jnp.concatenate([ref[at + (slice(None), slice(j * D, (j + 1) * D))] for j in range(R)], axis=0)

    def q_heads(g):
        wide = q_ref[0, :, pl.ds(pl.multiple_of(g * (R * D), R * D), R * D)]
        return jnp.concatenate([wide[:, j * D : (j + 1) * D] for j in range(R)], axis=0)

    def block(g, slot, first=False):
        head = kv[slot, g, 0:HEAD, :].astype(F32)
        k = kv[slot, g, HEAD : HEAD + T, :]
        v = kv[slot, g, HEAD + T : HEAD + 2 * T, :]
        q4 = q_heads(g)
        do4 = heads(do, g)
        kpos = jnp.where(krow < half, head[0:1, :], head[8:9, :]) * half + kbase
        allowed = kpos <= qpos
        lse = jnp.concatenate(
            [lse_ref[0, pl.ds(g * R + j, 1), :] for j in range(R)], axis=1
        ) * math.log2(math.e)
        dl = delta[g, 0:1, :]
        s = dot(k, q4, 1, 1)
        e = jnp.exp2(s * scale2 - lse)
        p = jnp.where(jnp.concatenate([allowed] * R, axis=1), e, 0.0)
        dp = dot(v, do4, 1, 1)
        ds = (p * (dp - dl) * scale).astype(BF16)
        dval = dot(p.astype(BF16), do4, 1, 0)
        dkey = dot(ds, q4, 1, 0)
        term = dot(k, ds, 0, 0)
        if first:
            dqt[g] = term
        else:
            dqt[g] += term
        return dkey, dval

    def keep(g, slot, pair):
        pacc[slot, g, 0:T, :] = pair[0]
        pacc[slot, g, T : 2 * T, :] = pair[1]

    def pass_on(t, g, pair):
        gsend[t, g, 0:T, :] = pair[0].astype(BF16)
        gsend[t, g, T : 2 * T, :] = pair[1].astype(BF16)
        g_copy(t, g).start()

    def relay(g):
        kv_copy(C1, 0, g).wait_recv()
        kv_copy(C2, 1, g).start()

        @pl.when(side == 0)
        def _():
            kv_copy(X3, 1, g).start()

        @pl.when(side == 1)
        def _():
            kv_copy(X1, 1, g).start()

        if g + AHEAD < G:
            send_own(g + AHEAD)

    def relay2(g):
        kv_copy(C2, 1, g).wait_recv()

        @pl.when(side == 1)
        def _():
            kv_copy(X3, 2, g).start()

    def work(g):
        up_copy(g).wait_recv()
        o4 = o_ref[0, :, pl.ds(pl.multiple_of(g * (R * D), R * D), R * D)].astype(F32)
        prod = o4 * do[g].astype(F32)
        delta[g, 0:1, :] = jnp.concatenate(
            [jnp.sum(prod[:, j * D : (j + 1) * D].T, axis=0, keepdims=True) for j in range(R)], axis=1
        )
        keep(g, 0, block(g, 0, True))
        keep(g, 1, block(g, 1))
        keep(g, 2, block(g, 2))
        kv_copy(X1, 0, g).wait_recv()
        pass_on(X1, g, block(g, 3))
        kv_copy(X3, 0, g).wait_recv()
        pass_on(X3, g, block(g, 4))
        total = dqt[g]
        dq_ref[0, :, pl.ds(pl.multiple_of(g * (R * D), R * D), R * D)] = jnp.concatenate(
            [total[:, j * T : (j + 1) * T].T for j in range(R)], axis=1
        ).astype(BF16)

    def join(g):
        g_copy(X1, g).wait_recv()
        pacc[side, g] += grecv[X1, g].astype(F32)
        g_copy(X3, g).wait_recv()
        pacc[side + 1, g] += grecv[X3, g].astype(F32)
        gsend[C2, g] = pacc[2, g].astype(BF16)
        g_copy(C2, g).start()

    def descend(g):
        g_copy(C2, g).wait_recv()
        gsend[C1, g] = (pacc[1, g] + grecv[C2, g].astype(F32)).astype(BF16)
        g_copy(C1, g).start()

    def home(g):
        g_copy(C1, g).wait_recv()
        total = (pacc[0, g] + grecv[C1, g].astype(F32)).astype(BF16)
        at = pl.ds(pl.multiple_of(g * D, D), D)
        dk_ref[0, :, at] = total[0:T]
        dv_ref[0, :, at] = total[T : 2 * T]

    stages = {"a": relay, "b": relay2, "w": work, "j": join, "d": descend, "h": home}
    for name, g in ORDER:
        stages[name](g)

    def finish(g, carry):
        up_copy(g).wait_send()
        for t in (C1, C2, X1, X3):
            kv_copy(t, 0, g).wait_send()
            g_copy(t, g).wait_send()
        return carry

    lax.fori_loop(0, G, finish, 0)


def body(mesh, queries, keys, values, outputs, upstream, lse, span_ids):
    T = queries.shape[1]
    rows = HEAD + 2 * T
    vmem = pl.BlockSpec(memory_space=pltpu.VMEM)
    return pl.pallas_call(
        functools.partial(kernel, mesh.shape["section"], mesh.shape["ctx"]),
        out_shape=(
            jax.ShapeDtypeStruct(queries.shape, BF16),
            jax.ShapeDtypeStruct(keys.shape, BF16),
            jax.ShapeDtypeStruct(values.shape, BF16),
        ),
        in_specs=[pl.BlockSpec(memory_space=pltpu.SMEM)] + [pl.BlockSpec(memory_space=pltpu.HBM)] * 6,
        out_specs=(vmem, vmem, vmem),
        scratch_shapes=[
            pltpu.VMEM(queries.shape, BF16),
            pltpu.VMEM(outputs.shape, BF16),
            pltpu.VMEM(lse.shape, F32),
            pltpu.VMEM((5, G, rows, D), BF16),
            pltpu.VMEM((G, T, R * D), BF16),
            pltpu.VMEM((G, D, R * T), F32),
            pltpu.VMEM((G, 8, R * T), F32),
            pltpu.VMEM((3, G, 2 * T, D), F32),
            pltpu.VMEM((4, G, 2 * T, D), BF16),
            pltpu.VMEM((4, G, 2 * T, D), BF16),
            pltpu.SemaphoreType.DMA((3,)),
            pltpu.SemaphoreType.DMA((2, G)),
            pltpu.SemaphoreType.DMA((G,)),
            pltpu.SemaphoreType.DMA((G,)),
            pltpu.SemaphoreType.DMA((4, G)),
            pltpu.SemaphoreType.DMA((4, G)),
            pltpu.SemaphoreType.DMA((4, G)),
            pltpu.SemaphoreType.DMA((4, G)),
        ],
        compiler_params=pltpu.CompilerParams(
            collective_id=0, has_side_effects=True, vmem_limit_bytes=60 * 1024 * 1024
        ),
    )(span_ids, queries, keys, values, outputs, lse, upstream)


def solution(mesh):
    placed = (
        P("section", "ctx", None),
        P("section", "ctx", None),
        P("section", "ctx", None),
        P("section", "ctx", None),
        P("section", "ctx", None),
        P("section", None, "ctx"),
        P("ctx"),
    )
    return jax.shard_map(
        functools.partial(body, mesh),
        mesh=mesh,
        in_specs=placed,
        out_specs=(P("section", "ctx", None), P("section", "ctx", None), P("section", "ctx", None)),
        check_vma=False,
    )
```

```python
import functools
import math

import jax
import jax.numpy as jnp
from jax import lax
from jax.experimental import pallas as pl
from jax.experimental.pallas import tpu as pltpu
from jax.sharding import PartitionSpec as P

G = 4
R = 4
D = 128
AHEAD = 4
HEAD = 16
ORDER = (
    ("a", 0), ("a", 1), ("a", 2), ("a", 3), ("b", 0), ("b", 1), ("b", 2), ("b", 3), ("w", 0), ("w", 1), ("w", 2), ("j", 0), ("w", 3), ("j", 1), ("d", 0), ("j", 2), ("d", 1), ("j", 3), ("d", 2), ("h", 0), ("d", 3), ("h", 1), ("h", 2), ("h", 3),
)
MESH = pl.DeviceIdType.MESH
F32 = jnp.float32
BF16 = jnp.bfloat16
C1, C2, X1, X3 = 0, 1, 2, 3


def dot(a, b, ca, cb):
    return lax.dot_general(a, b, (((ca,), (cb,)), ((), ())), preferred_element_type=F32)


def kernel(
    sections, count, span_ref, q_hbm, k_hbm, v_hbm, o_hbm, lse_hbm, up_ref,
    dq_ref, dk_ref, dv_ref,
    q_ref, o_ref, lse_ref,
    kv, do, dqt, delta, pacc, gsend, grecv,
    loc, kvloc, up_s, up_r, kv_s, kv_r, g_s, g_r,
):
    T = q_ref.shape[1]
    half = T // 2
    sec = lax.axis_index("section")
    me = lax.axis_index("ctx")
    side = lax.rem(me, 2)
    sec_prev = lax.rem(sec + sections - 1, sections)
    sec_next = lax.rem(sec + 1, sections)
    above = lax.rem(me + 2, count)
    below = lax.rem(me + count - 2, count)
    partner = me + 1 - 2 * side

    barrier = pltpu.get_barrier_semaphore()
    for axis, other in (
        ("ctx", above), ("ctx", below), ("ctx", partner),
        ("section", sec_prev), ("section", sec_next),
    ):
        pl.semaphore_signal(barrier, inc=1, device_id={axis: other}, device_id_type=MESH)

    own = []
    for g in range(G):
        cols = slice(g * D, (g + 1) * D)
        own.append((
            pltpu.make_async_copy(k_hbm.at[0, :, cols], kv.at[0, g, HEAD : HEAD + T, :], kvloc.at[0, g]),
            pltpu.make_async_copy(v_hbm.at[0, :, cols], kv.at[0, g, HEAD + T : HEAD + 2 * T, :], kvloc.at[1, g]),
        ))
        own[g][0].start()
        own[g][1].start()
    local = (
        pltpu.make_async_copy(q_hbm, q_ref, loc.at[0]),
        pltpu.make_async_copy(o_hbm, o_ref, loc.at[1]),
        pltpu.make_async_copy(lse_hbm, lse_ref, loc.at[2]),
    )
    for copy in local:
        copy.start()

    s0 = span_ref[0]
    s1 = span_ref[1]
    rows = lax.broadcasted_iota(jnp.int32, (HEAD, D), 0)
    header = jnp.where(rows < HEAD // 2, s0, s1).astype(F32).astype(BF16)
    for g in range(G):
        kv[0, g, 0:HEAD, :] = header
    pl.semaphore_wait(barrier, 5)

    def up_copy(g):
        return pltpu.make_async_remote_copy(
            src_ref=up_ref.at[0, :, pl.ds(pl.multiple_of(g * (R * D), R * D), R * D)],
            dst_ref=do.at[g], send_sem=up_s.at[g], recv_sem=up_r.at[g],
            device_id={"section": sec_prev}, device_id_type=MESH,
        )

    def kv_copy(t, src, g):
        return pltpu.make_async_remote_copy(
            src_ref=kv.at[src, g], dst_ref=kv.at[t + 1, g],
            send_sem=kv_s.at[t, g], recv_sem=kv_r.at[t, g],
            device_id={"ctx": above if t in (C1, C2) else partner}, device_id_type=MESH,
        )

    def g_copy(t, g):
        return pltpu.make_async_remote_copy(
            src_ref=gsend.at[t, g], dst_ref=grecv.at[t, g],
            send_sem=g_s.at[t, g], recv_sem=g_r.at[t, g],
            device_id={"ctx": below if t in (C1, C2) else partner}, device_id_type=MESH,
        )

    def send_own(g):
        kv_copy(C1, 0, g).start()

        @pl.when(side == 0)
        def _():
            kv_copy(X1, 0, g).start()

    for g in range(G):
        own[g][0].wait()
        own[g][1].wait()
        if g < AHEAD:
            send_own(g)
        up_copy(g).start()
    for copy in local:
        copy.wait()

    scale = D ** (-0.5)
    scale2 = scale * math.log2(math.e)
    krow = lax.broadcasted_iota(jnp.int32, (T, D), 0)
    kbase = jnp.where(krow < half, krow, krow - half).astype(F32)
    qlane = lax.broadcasted_iota(jnp.int32, (T, T), 1)
    qpos = (jnp.where(qlane < half, s0, s1) * half).astype(F32) + jnp.where(
        qlane < half, qlane, qlane - half
    ).astype(F32)

    def heads(ref, *at):
        return jnp.concatenate([ref[at + (slice(None), slice(j * D, (j + 1) * D))] for j in range(R)], axis=0)

    def q_heads(g):
        wide = q_ref[0, :, pl.ds(pl.multiple_of(g * (R * D), R * D), R * D)]
        return jnp.concatenate([wide[:, j * D : (j + 1) * D] for j in range(R)], axis=0)

    def block(g, slot, first=False):
        head = kv[slot, g, 0:HEAD, :].astype(F32)
        k = kv[slot, g, HEAD : HEAD + T, :]
        v = kv[slot, g, HEAD + T : HEAD + 2 * T, :]
        q4 = q_heads(g)
        do4 = heads(do, g)
        kpos = jnp.where(krow < half, head[0:1, :], head[8:9, :]) * half + kbase
        allowed = kpos <= qpos
        lse = jnp.concatenate(
            [lse_ref[0, pl.ds(g * R + j, 1), :] for j in range(R)], axis=1
        ) * math.log2(math.e)
        dl = delta[g, 0:1, :]
        s = dot(k, q4, 1, 1)
        e = jnp.exp2(s * scale2 - lse)
        p = jnp.where(jnp.concatenate([allowed] * R, axis=1), e, 0.0)
        dp = dot(v, do4, 1, 1)
        ds = (p * (dp - dl) * scale).astype(BF16)
        dval = dot(p.astype(BF16), do4, 1, 0)
        dkey = dot(ds, q4, 1, 0)
        term = dot(k, ds, 0, 0)
        if first:
            dqt[g] = term
        else:
            dqt[g] += term
        return dkey, dval

    def keep(g, slot, pair):
        pacc[slot, g, 0:T, :] = pair[0]
        pacc[slot, g, T : 2 * T, :] = pair[1]

    def pass_on(t, g, pair):
        gsend[t, g, 0:T, :] = pair[0].astype(BF16)
        gsend[t, g, T : 2 * T, :] = pair[1].astype(BF16)
        g_copy(t, g).start()

    def relay(g):
        kv_copy(C1, 0, g).wait_recv()
        kv_copy(C2, 1, g).start()

        @pl.when(side == 0)
        def _():
            kv_copy(X3, 1, g).start()

        @pl.when(side == 1)
        def _():
            kv_copy(X1, 1, g).start()

        if g + AHEAD < G:
            send_own(g + AHEAD)

    def relay2(g):
        kv_copy(C2, 1, g).wait_recv()

        @pl.when(side == 1)
        def _():
            kv_copy(X3, 2, g).start()

    def work(g):
        up_copy(g).wait_recv()
        o4 = o_ref[0, :, pl.ds(pl.multiple_of(g * (R * D), R * D), R * D)].astype(F32)
        prod = o4 * do[g].astype(F32)
        delta[g, 0:1, :] = jnp.concatenate(
            [jnp.sum(prod[:, j * D : (j + 1) * D].T, axis=0, keepdims=True) for j in range(R)], axis=1
        )
        keep(g, 0, block(g, 0, True))
        keep(g, 1, block(g, 1))
        keep(g, 2, block(g, 2))
        kv_copy(X1, 0, g).wait_recv()
        pass_on(X1, g, block(g, 3))
        kv_copy(X3, 0, g).wait_recv()
        pass_on(X3, g, block(g, 4))
        total = dqt[g]
        dq_ref[0, :, pl.ds(pl.multiple_of(g * (R * D), R * D), R * D)] = jnp.concatenate(
            [total[:, j * T : (j + 1) * T].T for j in range(R)], axis=1
        ).astype(BF16)

    def join(g):
        g_copy(X1, g).wait_recv()
        pacc[side, g] += grecv[X1, g].astype(F32)
        g_copy(X3, g).wait_recv()
        pacc[side + 1, g] += grecv[X3, g].astype(F32)
        gsend[C2, g] = pacc[2, g].astype(BF16)
        g_copy(C2, g).start()

    def descend(g):
        g_copy(C2, g).wait_recv()
        gsend[C1, g] = (pacc[1, g] + grecv[C2, g].astype(F32)).astype(BF16)
        g_copy(C1, g).start()

    def home(g):
        g_copy(C1, g).wait_recv()
        total = (pacc[0, g] + grecv[C1, g].astype(F32)).astype(BF16)
        at = pl.ds(pl.multiple_of(g * D, D), D)
        dk_ref[0, :, at] = total[0:T]
        dv_ref[0, :, at] = total[T : 2 * T]

    stages = {"a": relay, "b": relay2, "w": work, "j": join, "d": descend, "h": home}
    for name, g in ORDER:
        stages[name](g)

    def finish(g, carry):
        up_copy(g).wait_send()
        for t in (C1, C2, X1, X3):
            kv_copy(t, 0, g).wait_send()
            g_copy(t, g).wait_send()
        return carry

    lax.fori_loop(0, G, finish, 0)


def body(mesh, queries, keys, values, outputs, upstream, lse, span_ids):
    T = queries.shape[1]
    rows = HEAD + 2 * T
    vmem = pl.BlockSpec(memory_space=pltpu.VMEM)
    return pl.pallas_call(
        functools.partial(kernel, mesh.shape["section"], mesh.shape["ctx"]),
        out_shape=(
            jax.ShapeDtypeStruct(queries.shape, BF16),
            jax.ShapeDtypeStruct(keys.shape, BF16),
            jax.ShapeDtypeStruct(values.shape, BF16),
        ),
        in_specs=[pl.BlockSpec(memory_space=pltpu.SMEM)] + [pl.BlockSpec(memory_space=pltpu.HBM)] * 6,
        out_specs=(vmem, vmem, vmem),
        scratch_shapes=[
            pltpu.VMEM(queries.shape, BF16),
            pltpu.VMEM(outputs.shape, BF16),
            pltpu.VMEM(lse.shape, F32),
            pltpu.VMEM((5, G, rows, D), BF16),
            pltpu.VMEM((G, T, R * D), BF16),
            pltpu.VMEM((G, D, R * T), F32),
            pltpu.VMEM((G, 8, R * T), F32),
            pltpu.VMEM((3, G, 2 * T, D), F32),
            pltpu.VMEM((4, G, 2 * T, D), BF16),
            pltpu.VMEM((4, G, 2 * T, D), BF16),
            pltpu.SemaphoreType.DMA((3,)),
            pltpu.SemaphoreType.DMA((2, G)),
            pltpu.SemaphoreType.DMA((G,)),
            pltpu.SemaphoreType.DMA((G,)),
            pltpu.SemaphoreType.DMA((4, G)),
            pltpu.SemaphoreType.DMA((4, G)),
            pltpu.SemaphoreType.DMA((4, G)),
            pltpu.SemaphoreType.DMA((4, G)),
        ],
        compiler_params=pltpu.CompilerParams(
            collective_id=0, has_side_effects=True, vmem_limit_bytes=60 * 1024 * 1024
        ),
    )(span_ids, queries, keys, values, outputs, lse, upstream)


def solution(mesh):
    placed = (
        P("section", "ctx", None),
        P("section", "ctx", None),
        P("section", "ctx", None),
        P("section", "ctx", None),
        P("section", "ctx", None),
        P("section", None, "ctx"),
        P("ctx"),
    )
    return jax.shard_map(
        functools.partial(body, mesh),
        mesh=mesh,
        in_specs=placed,
        out_specs=(P("section", "ctx", None), P("section", "ctx", None), P("section", "ctx", None)),
        check_vma=False,
    )
```
